32 devices in a mesh: groups: 2 (over y), expert: 4 (over z), dp: 4 (over x, core).
Axes of the slice: x: 2, y: 2, z: 4, core: 2. Of those that a mesh axis runs over, the one named last changes fastest.
Arguments:
- tokens: bfloat16 [16384, 1024], P(('groups', 'expert', 'dp')), parts along dimension 0, may hold values from -100 to 100
- routes: int32 [16384, 2], P(('groups', 'expert', 'dp')), parts along dimension 0, may hold values from 0 to 3, all different within a row; in each aligned block of 512 rows (0 to 511, 512 to 1023, ...) at most 320 rows name the same one
- w_orig: float32 [4, 512, 1024], P('expert', 'dp'), may hold values from -6 to 6
- mask: int32 [4, 512, 1024], P('expert', 'dp'), may hold values from 0 to 1, as said below
Outputs:
- w_pruned: float32 [8, 512, 1024], P(('groups', 'expert'), 'dp'), parts along dimension 0
The draws below stay inside these ranges and needn't reach their ends.
There are 2 independent parts, one for each index of `groups`. The reference program is written for one: setup_inputs(seed, part) draws one part's arguments, and reference() takes and returns one part's arrays. A program takes and returns all parts, laid end to end along the dimension named above; an argument that names none is the same for every part. Nothing has to cross between parts.
Inputs may be any that keep to these rules, and one draw needn't show every extreme that they name: `routes`: in the rows of one device each expert is named by at most 320 rows, a bound that some block reaches; the 2 experts of a token differ. `mask`: each aligned group of four consecutive entries along the last dimension holds exactly two ones.
All inputs are finite; a program needn't handle non-finite values.
Results may differ from the reference program's by a relative error of at most 0.0008.
Values may be sent and summed in bfloat16 or wider, within the bound.
No kernel may reach another device: no remote copies, remote signals or barrier semaphores. Data moves between devices by JAX's collectives and lax.ppermute only.
A program may use at most 64 MiB of HBM per device.

```python
import math
import jax
import jax.numpy as jnp
import numpy as np
from jax import lax

FF = 1024
TOK_DEV = 512
STEPS = 3
EXPERTS = 4
TOPK = 2
CAP = 320
TOKENS = 8192
COLS = 512
N_EXPERT = 4
N_DP = 4


def draw_tokens(key, part):
    key = jax.random.fold_in(key, 5)
    key_feat, key_row, key_base = jax.random.split(key, 3)
    feature_scale = jnp.exp(jax.random.uniform(key_feat, (1, FF), jnp.float32, 0.0, math.log(10.0)))
    row_scale = jnp.exp(jax.random.uniform(key_row, (TOKENS, 1), jnp.float32, math.log(0.5), math.log(2.0)))
    base = jnp.clip(jax.random.normal(key_base, (TOKENS, FF), jnp.float32), -5.0, 5.0)
    values = base * feature_scale * row_scale
    return values.astype(jnp.bfloat16)


def draw_mask(key, part):
    key = jax.random.fold_in(key, 11)
    scores = jax.random.randint(key, (EXPERTS, COLS, FF // 4, 4), 0, 1 << 20) * 4 + jnp.arange(4, dtype=jnp.int32)
    ranks = jnp.argsort(jnp.argsort(scores, axis=-1), axis=-1)
    return (ranks < 2).astype(jnp.int32).reshape(EXPERTS, COLS, FF)


def block_levels(rng, extent, pieces, low, top_value):
    loudness, own = 1.0, jax.random.fold_in(rng, 6)
    for axis_at, blocks in pieces:
        draws = jnp.exp(jax.random.uniform(jax.random.fold_in(own, axis_at), (blocks,), jnp.float32, low / len(pieces), top_value / len(pieces)))
        loudness = loudness * jnp.repeat(draws, extent[axis_at] // blocks).reshape([-1 if axis == axis_at else 1 for axis in range(len(extent))])
    return loudness


def deal_out(rng, own, number, rows, amount, top, reach, skew):
    ranking = jax.random.permutation(rng, amount)
    packed, usual = load_shares(amount, rows * top, reach, skew, True), load_shares(amount, rows * top, reach, skew, False)
    places = jnp.arange(amount)

    def named(tallies, rotation):
        used = int((tallies > 0).sum())
        fixed = max(1, used // 4)
        shifted = fixed + (places - fixed + rotation * (used - fixed)) % max(1, amount - fixed)
        return jnp.zeros((amount,), jnp.int32).at[ranking[jnp.where(places < fixed, places, shifted)]].set(jnp.asarray(tallies, jnp.int32))

    tallies = jnp.where(number % 4 == 0, named(packed, number // 4), named(usual, number - number // 4 - 1))
    mixed = jax.random.permutation(jax.random.fold_in(own, 3), amount)
    donor, taker = mixed[0:amount // 2 * 2:2], mixed[1:amount // 2 * 2:2]
    room = jnp.minimum(tallies[donor] - 1, reach - tallies[taker]) // 2
    room = jnp.where((donor == ranking[0]) | (taker == ranking[0]) | (tallies[taker] == 0), 0, jnp.maximum(room, 0))
    shifted = jax.random.randint(jax.random.fold_in(own, 4), (amount // 2,), 0, 1 << 20) % (room + 1)
    tallies = tallies.at[donor].add(-shifted).at[taker].add(shifted)
    labels = jnp.searchsorted(jnp.cumsum(tallies), jnp.arange(rows * top), side="right").astype(jnp.int32)
    listing = labels.reshape(top, rows).T
    listing = listing[jax.random.permutation(jax.random.fold_in(own, 1), rows)]
    rotation = jax.random.randint(jax.random.fold_in(own, 2), (rows, 1), 0, top)
    return jnp.take_along_axis(listing, (jnp.arange(top)[None, :] + rotation) % top, axis=1)


def load_shares(count, total, reach, slope, full):
    portions = [(1 << 20) // math.isqrt(standing ** slope) + 1 for standing in range(1, count + 1)]
    largest = reach if full else min(reach, max(-(-total // count), total * portions[0] // sum(portions)))
    least = 1 if total - largest >= count - 1 else 0
    given, spare = [largest] + [least] * (count - 1), total - largest - least * (count - 1)
    while spare > 0:
        free = [i for i in range(1, count) if given[i] < largest] or [i for i in range(1, count) if given[i] < reach]
        pool, remaining = sum([portions[i] for i in free]), spare
        for i in free:
            extra = min(reach - given[i], max(1, remaining * portions[i] // pool), spare)
            given[i] = given[i] + extra
            spare = spare - extra
    return np.array(given)


def normal_values(stream_key, dims, width, bound, shards=(), kind=jnp.bfloat16):
    result = width * jax.random.normal(stream_key, dims, jnp.float32)
    if shards:
        result = result * block_levels(stream_key, dims, shards, -0.22, 0.18)
    return jnp.clip(result, -bound, bound).astype(kind)


def setup_inputs(seed: int = 0, part: int = 0) -> dict:
    splits = jax.random.split(jax.random.key(seed), 5)
    part_keys = jax.random.split(jax.random.fold_in(splits[4], part), 5)
    tokens = draw_tokens(jax.random.fold_in(jax.random.fold_in(splits[4], part), 71), part)
    routes_keys = jax.random.split(jax.random.fold_in(part_keys[1], 1), TOKENS // TOK_DEV)
    routes_turns = jax.random.permutation(jax.random.fold_in(part_keys[1], 3), TOKENS // TOK_DEV)
    routes = jax.vmap(lambda own, number: deal_out(jax.random.fold_in(part_keys[1], 2), own, number, TOK_DEV, EXPERTS, TOPK, CAP, 2))(routes_keys, routes_turns).reshape((TOKENS, TOPK))
    w_orig = normal_values(splits[2], (EXPERTS, COLS, FF), 1.0, 6.0, ((0, 4), (1, 4)), jnp.float32)
    mask = draw_mask(jax.random.fold_in(splits[4], 71), part)
    return {"tokens": tokens, "routes": routes, "w_orig": w_orig, "mask": mask}


step_scale = 1.5

def reference(tokens, routes, w_orig, mask):
    flat_routes = routes.reshape(-1).astype(jnp.int32)
    ordering = jnp.argsort(flat_routes, stable=True).astype(jnp.int32)
    counts = jnp.zeros((EXPERTS,), jnp.int32).at[flat_routes].add(1)
    starts = (jnp.cumsum(counts) - counts).astype(jnp.int32)
    longest = CAP * N_EXPERT * N_DP
    padded = jnp.concatenate([ordering, jnp.zeros((longest,), jnp.int32)])
    positions = jnp.arange(longest, dtype=jnp.int32)

    def one_expert(expert):
        picked = lax.dynamic_slice(padded, (starts[expert],), (longest,))
        valid = (positions < counts[expert]).astype(jnp.float32)
        token_rows = (picked // TOPK).astype(jnp.int32)
        rows = tokens[token_rows].astype(jnp.float32) * valid[:, None]
        gram_matrix = lax.dot_general(rows, rows, (((0,), (0,)), ((), ())), precision=lax.Precision.HIGHEST, preferred_element_type=jnp.float32)
        frobenius = jnp.sqrt(jnp.sum(gram_matrix * gram_matrix) + 1e-06)
        rate_value = step_scale / frobenius
        dense_copy = w_orig[expert]
        keep_mask = mask[expert].astype(jnp.float32)
        weights = keep_mask * dense_copy
        for section in range(STEPS):
            change = weights - dense_copy
            gradient = jnp.dot(change, gram_matrix, precision=lax.Precision.HIGHEST, preferred_element_type=jnp.float32)
            weights = keep_mask * (weights - rate_value * gradient)
        return weights
    return lax.map(one_expert, jnp.arange(EXPERTS, dtype=jnp.int32))
```

```python
import functools

import jax
import jax.numpy as jnp
from jax import lax
from jax.experimental import pallas as pl
from jax.experimental.pallas import tpu as pltpu
from jax.sharding import PartitionSpec as P

STEPS = 3


step_scale = 1.5

BLK = 128
PIECE = 32
VMEM = pl.BlockSpec(memory_space=pltpu.VMEM)
SMEM = pl.BlockSpec(memory_space=pltpu.SMEM)


def full_product(rows):
    return lax.dot_general(rows, rows, (((0,), (0,)), ((), ())), preferred_element_type=jnp.float32)


def local_rows(tokens, routes, w_orig, mask):
    experts_n = lax.axis_size("expert")
    tok_rows, topk_count = routes.shape
    width = tokens.shape[1]
    capacity = max(2, min(tok_rows, 5 * tok_rows * topk_count // (4 * experts_n)))
    flat_routes = routes.reshape(-1)
    onehot = (flat_routes[:, None] == jnp.arange(experts_n, dtype=jnp.int32)[None, :]).astype(
        jnp.int32
    )
    before = jnp.cumsum(onehot, axis=0) - onehot
    slot_index = jnp.sum(before * onehot, axis=1)
    target = flat_routes * capacity + slot_index
    source = jnp.arange(flat_routes.shape[0], dtype=jnp.int32) // topk_count
    buffer = jnp.zeros((experts_n * capacity, width), jnp.bfloat16).at[target].set(tokens[source])
    outgoing = buffer.reshape(experts_n, capacity, width)
    arrived = lax.all_to_all(outgoing, "expert", split_axis=0, concat_axis=0, tiled=True).reshape(
        experts_n * capacity, width
    )
    local_terms = full_product(arrived)
    gram_matrix = lax.psum(local_terms.astype(jnp.bfloat16), "dp").astype(jnp.float32)
    frobenius = jnp.sqrt(jnp.sum(gram_matrix * gram_matrix) + 1e-06)
    rate_value = step_scale / frobenius
    dense_copy = w_orig[0]
    keep_mask = mask[0].astype(jnp.float32)
    weights = keep_mask * dense_copy
    for section in range(STEPS):
        change = weights - dense_copy
        gradient = jnp.dot(
            change, gram_matrix, precision=lax.Precision.HIGHEST, preferred_element_type=jnp.float32
        )
        weights = keep_mask * (weights - rate_value * gradient)
    return weights[None]


def turn_kernel(where, tokens, routes_t, out):
    width = tokens.shape[1]
    out[0:width, :] = tokens[...].T
    experts = lax.broadcasted_iota(jnp.int32, (16, tokens.shape[0]), 0) ^ where[0]
    named = experts == routes_t[0:1, :]
    for k in range(1, routes_t.shape[0]):
        named = named | (experts == routes_t[k : k + 1, :])
    out[width : width + 16, :] = named.astype(jnp.float32).astype(jnp.bfloat16)


def gram_kernel(panels, experts, where, mine, other, keep, send, lhs):
    width = mine.shape[0] - 16
    toks = mine.shape[1]
    group = 2 * experts * PIECE
    row = 64 * where[2]
    at_keep = row + PIECE * where[1]
    at_send = row + PIECE * (1 - where[1])
    blocks = 2 * max(panels) + 2
    for half, source in enumerate((mine, other)):
        flags = source[width : width + 16, :]
        lanes = slice(half * toks, (half + 1) * toks)
        for k in range(blocks):
            for s, at in enumerate((at_keep, at_send)):
                rows = source[pl.ds(pl.multiple_of(at + BLK * k, PIECE), PIECE), :]
                for e in range(experts):
                    first = group * k + experts * PIECE * s + PIECE * e
                    lhs[first : first + PIECE, lanes] = rows * flags[e : e + 1, :]
    base = 0
    for j in panels:
        used = lhs[0 : group * (2 * j + 2), :]
        total = lax.dot_general(
            used[:, 0:toks], mine[256 * j : 256 * j + 256, :], (((1,), (1,)), ((), ())),
            preferred_element_type=jnp.float32)
        total = total + lax.dot_general(
            used[:, toks:], other[256 * j : 256 * j + 256, :], (((1,), (1,)), ((), ())),
            preferred_element_type=jnp.float32)
        for side in range(2):
            for k in range(2 * j + side + 1):
                for s, out in enumerate((keep, send)):
                    for e in range(experts):
                        first = group * k + experts * PIECE * s + PIECE * e
                        out[e, base + PIECE * k : base + PIECE * (k + 1), :] = total[
                            first : first + PIECE, BLK * side : BLK * (side + 1)].astype(out.dtype)
            base += PIECE * (2 * j + side + 1)


def pair_kernel(keep, got, own, *outs):
    for e, out in enumerate((own,) + outs):
        out[...] = (keep[e] + got[e].astype(jnp.float32)).astype(out.dtype)


def sum_kernel(own, *refs):
    total = own[...]
    for ref in refs[:-1]:
        total = total + ref[...].astype(jnp.float32)
    refs[-1][...] = total.astype(jnp.bfloat16)


def steps_kernel(chunks, where, w_ref, mask_ref, *refs):
    pieces, (out, gram) = refs[:-2], refs[-2:]
    width = w_ref.shape[1]
    core, x = where[2], where[1]
    ats = (64 * core + PIECE * x, 64 * (1 - core) + PIECE * x,
           64 * core + PIECE * (1 - x), 64 * (1 - core) + PIECE * (1 - x))
    square = jnp.zeros((PIECE, BLK), jnp.float32)
    n = 0
    for panels in chunks:
        for at in ats:
            piece, base = pieces[n], 0
            n += 1
            for j in panels:
                for c in (2 * j, 2 * j + 1):
                    for k in range(c + 1):
                        block = piece[base : base + PIECE, :]
                        base += PIECE
                        gram[pl.ds(pl.multiple_of(at + BLK * k, PIECE), PIECE), BLK * c : BLK * (c + 1)] = block
                        value = block.astype(jnp.float32)
                        square = square + value * value * (1.0 if k == c else 2.0)
    for c in range(width // BLK):
        for k in range(c):
            gram[BLK * c : BLK * (c + 1), BLK * k : BLK * (k + 1)] = gram[
                BLK * k : BLK * (k + 1), BLK * c : BLK * (c + 1)].T
    rate = step_scale / jnp.sqrt(jnp.sum(square) + 1e-06)
    dense = w_ref[...]
    keep = mask_ref[...].astype(jnp.float32)
    weights = keep * dense
    rows = dense.shape[0]
    for section in range(STEPS):
        change = weights - dense
        high = change.astype(jnp.bfloat16)
        low = (change - high.astype(jnp.float32)).astype(jnp.bfloat16)
        both = jnp.dot(jnp.concatenate([high, low], axis=0), gram[...], preferred_element_type=jnp.float32)
        weights = keep * (weights - rate * (both[0:rows] + both[rows:]))
    out[...] = weights


def params(mib=48):
    return pltpu.CompilerParams(vmem_limit_bytes=mib << 20)


def local_grams(chunks, tokens, routes, w_orig, mask):
    toks, width = tokens.shape
    experts = lax.axis_size("expert")
    z, dp = lax.axis_index("expert"), lax.axis_index("dp")
    where = jnp.stack([z, dp // 2, dp % 2]).astype(jnp.int32)
    over_core = [(d, d ^ 1) for d in range(4)]
    over_x = [(d, d ^ 2) for d in range(4)]
    bf16, f32 = jnp.bfloat16, jnp.float32
    turned = pl.pallas_call(
        turn_kernel, in_specs=[SMEM, VMEM, VMEM], out_specs=VMEM,
        out_shape=jax.ShapeDtypeStruct((width + 16, toks), bf16), compiler_params=params(),
    )(where, tokens, routes.T)
    other = lax.ppermute(turned, "dp", over_core)
    pieces = []
    for panels in chunks:
        rows = PIECE * sum(4 * j + 3 for j in panels)
        keep, send = pl.pallas_call(
            functools.partial(gram_kernel, panels, experts),
            in_specs=[SMEM, VMEM, VMEM], out_specs=[VMEM, VMEM],
            out_shape=[jax.ShapeDtypeStruct((experts, rows, BLK), f32),
                       jax.ShapeDtypeStruct((experts, rows, BLK), bf16)],
            scratch_shapes=[pltpu.VMEM((2 * experts * PIECE * (2 * max(panels) + 2), 2 * toks), bf16)],
            compiler_params=params(),
        )(where, turned, other)
        got = lax.ppermute(send, "dp", over_x)
        own, *away = pl.pallas_call(
            pair_kernel, in_specs=[VMEM] * 2, out_specs=[VMEM] * experts,
            out_shape=[jax.ShapeDtypeStruct((rows, BLK), f32)]
            + [jax.ShapeDtypeStruct((rows, BLK), bf16)] * (experts - 1),
            compiler_params=params(),
        )(keep, got)
        came = [lax.ppermute(a, "expert", [(i, i ^ (s + 1)) for i in range(experts)])
                for s, a in enumerate(away)]
        final = pl.pallas_call(
            sum_kernel, in_specs=[VMEM] * experts, out_specs=VMEM,
            out_shape=jax.ShapeDtypeStruct((rows, BLK), bf16), compiler_params=params(),
        )(own, *came)
        by_core = lax.ppermute(final, "dp", over_core)
        by_x = lax.ppermute(final, "dp", over_x)
        by_both = lax.ppermute(by_x, "dp", over_core)
        pieces += [final, by_core, by_x, by_both]
    out = pl.pallas_call(
        functools.partial(steps_kernel, chunks),
        in_specs=[SMEM] + [VMEM] * (2 + len(pieces)), out_specs=VMEM,
        out_shape=jax.ShapeDtypeStruct(w_orig.shape[1:], f32),
        scratch_shapes=[pltpu.VMEM((width, width), bf16)], compiler_params=params(),
    )(where, w_orig[0], mask[0], *pieces)
    return out[None]


def solution(mesh):
    placed = (
        P(("groups", "expert", "dp"), None),
        P(("groups", "expert", "dp"), None),
        P("expert", "dp", None),
        P("expert", "dp", None),
    )
    few = mesh.shape["expert"] == 4 and mesh.shape["dp"] == 4
    local = functools.partial(local_grams, ((3,), (2,), (0, 1))) if few else local_rows
    return jax.shard_map(
        local,
        mesh=mesh,
        in_specs=placed,
        out_specs=P(("groups", "expert"), "dp", None),
        check_vma=False,
    )
```

```python
import functools

import jax
import jax.numpy as jnp
from jax import lax
from jax.experimental import pallas as pl
from jax.experimental.pallas import tpu as pltpu
from jax.sharding import PartitionSpec as P

STEPS = 3


step_scale = 1.5

BLK = 128
PIECE = 32
VMEM = pl.BlockSpec(memory_space=pltpu.VMEM)
SMEM = pl.BlockSpec(memory_space=pltpu.SMEM)


def full_product(rows):
    return lax.dot_general(rows, rows, (((0,), (0,)), ((), ())), preferred_element_type=jnp.float32)


def local_rows(tokens, routes, w_orig, mask):
    experts_n = lax.axis_size("expert")
    tok_rows, topk_count = routes.shape
    width = tokens.shape[1]
    capacity = max(2, min(tok_rows, 5 * tok_rows * topk_count // (4 * experts_n)))
    flat_routes = routes.reshape(-1)
    onehot = (flat_routes[:, None] == jnp.arange(experts_n, dtype=jnp.int32)[None, :]).astype(
        jnp.int32
    )
    before = jnp.cumsum(onehot, axis=0) - onehot
    slot_index = jnp.sum(before * onehot, axis=1)
    target = flat_routes * capacity + slot_index
    source = jnp.arange(flat_routes.shape[0], dtype=jnp.int32) // topk_count
    buffer = jnp.zeros((experts_n * capacity, width), jnp.bfloat16).at[target].set(tokens[source])
    outgoing = buffer.reshape(experts_n, capacity, width)
    arrived = lax.all_to_all(outgoing, "expert", split_axis=0, concat_axis=0, tiled=True).reshape(
        experts_n * capacity, width
    )
    local_terms = full_product(arrived)
    gram_matrix = lax.psum(local_terms.astype(jnp.bfloat16), "dp").astype(jnp.float32)
    frobenius = jnp.sqrt(jnp.sum(gram_matrix * gram_matrix) + 1e-06)
    rate_value = step_scale / frobenius
    dense_copy = w_orig[0]
    keep_mask = mask[0].astype(jnp.float32)
    weights = keep_mask * dense_copy
    for section in range(STEPS):
        change = weights - dense_copy
        gradient = jnp.dot(
            change, gram_matrix, precision=lax.Precision.HIGHEST, preferred_element_type=jnp.float32
        )
        weights = keep_mask * (weights - rate_value * gradient)
    return weights[None]


def count(panels):
    return sum(4 * j + 3 for j in panels)


def blocks_of(panels):
    return [(k, c) for j in panels for c in (2 * j, 2 * j + 1) for k in range(c + 1)]


def lift_kernel(experts, where, tokens, routes_t, out, turned):
    toks, width = tokens.shape
    turned[...] = tokens[...].T
    numbers = lax.broadcasted_iota(jnp.int32, (16, toks), 0) ^ where[0]
    named = numbers == routes_t[0:1, :]
    for k in range(1, routes_t.shape[0]):
        named = named | (numbers == routes_t[k : k + 1, :])
    flags = named.astype(jnp.float32).astype(jnp.bfloat16)
    row = 64 * where[2]
    ats = (row + PIECE * where[1], row + PIECE * (1 - where[1]))
    first = 0
    for k in range(width // BLK):
        for at in ats:
            rows = turned[pl.ds(pl.multiple_of(at + BLK * k, PIECE), PIECE), :]
            for e in range(experts):
                out[first : first + PIECE, :] = rows * flags[e : e + 1, :]
                first += PIECE


def gram_kernel(panels, mode, experts, where, lhs_a, tok_a, lhs_b, tok_b, keep, send):
    group = 2 * experts * PIECE
    halves = (PIECE * where[1], PIECE * (1 - where[1]))
    base = 0
    for j in panels:
        used, cols = slice(0, group * (2 * j + 2)), slice(256 * j, 256 * j + 256)
        total = jnp.dot(lhs_a[used, :], tok_a[:, cols], preferred_element_type=jnp.float32)
        total = total + jnp.dot(lhs_b[used, :], tok_b[:, cols], preferred_element_type=jnp.float32)
        for side in range(2):
            for k in range(2 * j + side + 1):
                for s in range(2):
                    for e in range(experts):
                        first = group * k + experts * PIECE * s + PIECE * e
                        value = total[first : first + PIECE, BLK * side : BLK * (side + 1)]
                        if mode == "z":
                            out = keep if e % 2 == 0 else send
                            at = pl.multiple_of(halves[s] + base, PIECE)
                            out[e // 2, pl.ds(at, PIECE), :] = value.astype(out.dtype)
                        else:
                            out = (keep, send)[s]
                            out[e, base : base + PIECE, :] = value.astype(out.dtype)
                base += 2 * PIECE if mode == "z" else PIECE


def pair_kernel(keep, got, own, *outs):
    for e, out in enumerate((own,) + outs):
        out[...] = (keep[e] + got[e].astype(jnp.float32)).astype(out.dtype)


def split_kernel(keep, got, own, out):
    for e in range(4):
        to = (own, out)[e % 2]
        to[e // 2] = (keep[e] + got[e].astype(jnp.float32)).astype(to.dtype)


def sum_kernel(*refs):
    total = refs[0][...].astype(jnp.float32)
    for ref in refs[1:-1]:
        total = total + ref[...].astype(jnp.float32)
    refs[-1][...] = total.astype(refs[-1].dtype)


def put_pieces(chunk, gram, where):
    panels, size, pieces = chunk
    core, x = where[2], where[1]
    if size == PIECE:
        ats = [64 * a + PIECE * b for b in (x, 1 - x) for a in (core, 1 - core)]
    else:
        ats = [64 * a for a in (core, 1 - core)]
    square = jnp.zeros((PIECE, BLK), jnp.float32)
    for at, piece in zip(ats, pieces):
        base = 0
        for k, c in blocks_of(panels):
            gram[pl.ds(pl.multiple_of(at + BLK * k, PIECE), size), BLK * c : BLK * (c + 1)] = piece[
                base : base + size, :]
            for part in range(0, size, PIECE):
                value = piece[base + part : base + part + PIECE, :].astype(jnp.float32)
                square = square + value * value * (1.0 if k == c else 2.0)
            base += size
    for k, c in blocks_of(panels):
        if k < c:
            gram[BLK * c : BLK * (c + 1), BLK * k : BLK * (k + 1)] = gram[
                BLK * k : BLK * (k + 1), BLK * c : BLK * (c + 1)].T
    return square


def unflatten(shape, refs):
    refs, out = list(refs), []
    for panels, size, pieces in shape:
        out.append((panels, size, refs[:pieces]))
        refs = refs[pieces:]
    return out


def early_kernel(shape, where, *refs):
    gram, square = refs[-2:]
    square[...] = sum(put_pieces(chunk, gram, where) for chunk in unflatten(shape, refs[:-2]))


def steps_kernel(shape, where, w_ref, mask_ref, old, square, *refs):
    pieces, (out, gram) = refs[:-2], refs[-2:]
    total = square[...] + sum(put_pieces(chunk, gram, where) for chunk in unflatten(shape, pieces))
    rate = step_scale / jnp.sqrt(jnp.sum(total) + 1e-06)
    dense = w_ref[...]
    keep = mask_ref[...].astype(jnp.float32)
    weights = keep * dense
    rows = dense.shape[0]
    for section in range(STEPS):
        change = weights - dense
        high = change.astype(jnp.bfloat16)
        low = (change - high.astype(jnp.float32)).astype(jnp.bfloat16)
        both = jnp.dot(jnp.concatenate([high, low], axis=0), gram[...], preferred_element_type=jnp.float32)
        weights = keep * (weights - rate * (both[0:rows] + both[rows:]))
    out[...] = weights


def call(kernel, outs, *args, scratch=(), smem=True, aliases={}):
    return pl.pallas_call(
        kernel, in_specs=[SMEM if smem and i == 0 else VMEM for i in range(len(args))],
        out_specs=[VMEM] * len(outs),
        out_shape=[jax.ShapeDtypeStruct(s, d) for s, d in outs],
        scratch_shapes=list(scratch), input_output_aliases=aliases,
        compiler_params=pltpu.CompilerParams(vmem_limit_bytes=16 << 20),
    )(*args)


def over(axis, bit):
    return lambda a: lax.ppermute(a, axis, [(i, i ^ bit) for i in range(4)])


def local_grams(plan, tokens, routes, w_orig, mask):
    toks, width = tokens.shape
    experts = lax.axis_size("expert")
    z, dp = lax.axis_index("expert"), lax.axis_index("dp")
    where = jnp.stack([z, dp // 2, dp % 2]).astype(jnp.int32)
    over_core, over_x = over("dp", 1), over("dp", 2)
    bf16, f32 = jnp.bfloat16, jnp.float32

    def lift(tok, routes_t):
        return call(functools.partial(lift_kernel, experts), [((2 * width, toks), bf16)],
                    where, tok, routes_t, scratch=[pltpu.VMEM((width, toks), bf16)])[0]

    other, other_routes = over_core(tokens), over_core(routes.T)
    lhs = lift(tokens, routes.T)
    other_lhs = lift(other, other_routes)
    shape, found = [], []
    for panels, mode in plan:
        blocks = count(panels)
        first = mode == "z"
        dims = (2, 2 * PIECE * blocks, BLK) if first else (experts, PIECE * blocks, BLK)
        keep, send = call(functools.partial(gram_kernel, panels, mode, experts),
                          [(dims, f32), (dims, bf16)], where, lhs, tokens, other_lhs, other)
        size = 2 * PIECE if first else PIECE
        flat = (size * blocks, BLK)
        if not first:
            got = over_x(send)
        if mode == "direct":
            own, *away = call(pair_kernel, [(flat, f32)] + [(flat, bf16)] * (experts - 1), keep, got, smem=False)
            came = [over("expert", s + 1)(a) for s, a in enumerate(away)]
            final = call(sum_kernel, [(flat, bf16)], own, *came, smem=False)[0]
        else:
            if not first:
                keep, send = call(split_kernel, [((2,) + flat, f32), ((2,) + flat, bf16)], keep, got, smem=False)
            near = over("expert", 1)(send)
            own, away = call(pair_kernel, [(flat, f32), (flat, bf16)], keep, near, smem=False)
            far = over("expert", 2)(away)
            final = call(sum_kernel, [(flat, bf16)], own, far, smem=False)[0]
        if first:
            final = call(sum_kernel, [(flat, bf16)], final, over_x(final), smem=False)[0]
            pieces = [final, over_core(final)]
        else:
            by_x = over_x(final)
            pieces = [final, over_core(final), by_x, over_core(by_x)]
        shape.append((panels, size, len(pieces)))
        found.append(pieces)
    gram, square = call(functools.partial(early_kernel, tuple(shape[:-1])),
                        [((width, width), bf16), ((PIECE, BLK), f32)],
                        where, *[p for pieces in found[:-1] for p in pieces])
    out, _ = call(functools.partial(steps_kernel, tuple(shape[-1:])),
                  [(w_orig.shape[1:], f32), ((width, width), bf16)],
                  where, w_orig[0], mask[0], gram, square, *found[-1], aliases={3: 1})
    return out[None]


PLAN = (((2,), "z"), ((3,), "direct"), ((0, 1), "direct"))


def solution(mesh):
    placed = (
        P(("groups", "expert", "dp"), None),
        P(("groups", "expert", "dp"), None),
        P("expert", "dp", None),
        P("expert", "dp", None),
    )
    few = mesh.shape["expert"] == 4 and mesh.shape["dp"] == 4
    local = functools.partial(local_grams, PLAN) if few else local_rows
    return jax.shard_map(
        local,
        mesh=mesh,
        in_specs=placed,
        out_specs=P(("groups", "expert"), "dp", None),
        check_vma=False,
    )
```

```python
import functools

import jax
import jax.numpy as jnp
from jax import lax
from jax.experimental import pallas as pl
from jax.experimental.pallas import tpu as pltpu
from jax.sharding import PartitionSpec as P

STEPS = 3


step_scale = 1.5

BLK = 128
PIECE = 32
VMEM = pl.BlockSpec(memory_space=pltpu.VMEM)
SMEM = pl.BlockSpec(memory_space=pltpu.SMEM)


def full_product(rows):
    return lax.dot_general(rows, rows, (((0,), (0,)), ((), ())), preferred_element_type=jnp.float32)


def local_rows(tokens, routes, w_orig, mask):
    experts_n = lax.axis_size("expert")
    tok_rows, topk_count = routes.shape
    width = tokens.shape[1]
    capacity = max(2, min(tok_rows, 5 * tok_rows * topk_count // (4 * experts_n)))
    flat_routes = routes.reshape(-1)
    onehot = (flat_routes[:, None] == jnp.arange(experts_n, dtype=jnp.int32)[None, :]).astype(
        jnp.int32
    )
    before = jnp.cumsum(onehot, axis=0) - onehot
    slot_index = jnp.sum(before * onehot, axis=1)
    target = flat_routes * capacity + slot_index
    source = jnp.arange(flat_routes.shape[0], dtype=jnp.int32) // topk_count
    buffer = jnp.zeros((experts_n * capacity, width), jnp.bfloat16).at[target].set(tokens[source])
    outgoing = buffer.reshape(experts_n, capacity, width)
    arrived = lax.all_to_all(outgoing, "expert", split_axis=0, concat_axis=0, tiled=True).reshape(
        experts_n * capacity, width
    )
    local_terms = full_product(arrived)
    gram_matrix = lax.psum(local_terms.astype(jnp.bfloat16), "dp").astype(jnp.float32)
    frobenius = jnp.sqrt(jnp.sum(gram_matrix * gram_matrix) + 1e-06)
    rate_value = step_scale / frobenius
    dense_copy = w_orig[0]
    keep_mask = mask[0].astype(jnp.float32)
    weights = keep_mask * dense_copy
    for section in range(STEPS):
        change = weights - dense_copy
        gradient = jnp.dot(
            change, gram_matrix, precision=lax.Precision.HIGHEST, preferred_element_type=jnp.float32
        )
        weights = keep_mask * (weights - rate_value * gradient)
    return weights[None]


def count(panels):
    return sum(4 * j + 3 for j in panels)


def blocks_of(panels):
    return [(k, c) for j in panels for c in (2 * j, 2 * j + 1) for k in range(c + 1)]


def lift_kernel(experts, where, tokens, routes_t, out, turned):
    toks, width = tokens.shape
    turned[...] = tokens[...].T
    numbers = lax.broadcasted_iota(jnp.int32, (16, toks), 0) ^ where[0]
    named = numbers == routes_t[0:1, :]
    for k in range(1, routes_t.shape[0]):
        named = named | (numbers == routes_t[k : k + 1, :])
    flags = named.astype(jnp.float32).astype(jnp.bfloat16)
    row = 64 * where[2]
    ats = (row + PIECE * where[1], row + PIECE * (1 - where[1]))
    first = 0
    for k in range(width // BLK):
        for at in ats:
            rows = turned[pl.ds(pl.multiple_of(at + BLK * k, PIECE), PIECE), :]
            for e in range(experts):
                out[first : first + PIECE, :] = rows * flags[e : e + 1, :]
                first += PIECE


def gram_kernel(panels, mode, experts, where, lhs_a, tok_a, lhs_b, tok_b, keep, send):
    group = 2 * experts * PIECE
    halves = (PIECE * where[1], PIECE * (1 - where[1]))
    base = 0
    for j in panels:
        used, cols = slice(0, group * (2 * j + 2)), slice(256 * j, 256 * j + 256)
        total = jnp.dot(lhs_a[used, :], tok_a[:, cols], preferred_element_type=jnp.float32)
        total = total + jnp.dot(lhs_b[used, :], tok_b[:, cols], preferred_element_type=jnp.float32)
        for side in range(2):
            for k in range(2 * j + side + 1):
                for s in range(2):
                    for e in range(experts):
                        first = group * k + experts * PIECE * s + PIECE * e
                        value = total[first : first + PIECE, BLK * side : BLK * (side + 1)]
                        if mode == "z":
                            out = keep if e % 2 == 0 else send
                            at = pl.multiple_of(halves[s] + base, PIECE)
                            out[e // 2, pl.ds(at, PIECE), :] = value.astype(out.dtype)
                        else:
                            out = (keep, send)[s]
                            out[e, base : base + PIECE, :] = value.astype(out.dtype)
                base += 2 * PIECE if mode == "z" else PIECE


def pair_kernel(keep, got, own, *outs):
    for e, out in enumerate((own,) + outs):
        out[...] = (keep[e] + got[e].astype(jnp.float32)).astype(out.dtype)


def split_kernel(keep, got, own, out):
    for e in range(4):
        to = (own, out)[e % 2]
        to[e // 2] = (keep[e] + got[e].astype(jnp.float32)).astype(to.dtype)


def sum_kernel(*refs):
    total = refs[0][...].astype(jnp.float32)
    for ref in refs[1:-1]:
        total = total + ref[...].astype(jnp.float32)
    refs[-1][...] = total.astype(refs[-1].dtype)


def put_pieces(chunk, gram, where):
    panels, size, pieces = chunk
    core, x = where[2], where[1]
    if size == PIECE:
        ats = [64 * a + PIECE * b for b in (x, 1 - x) for a in (core, 1 - core)]
    else:
        ats = [64 * a for a in (core, 1 - core)]
    square = jnp.zeros((PIECE, BLK), jnp.float32)
    for at, piece in zip(ats, pieces):
        base = 0
        for k, c in blocks_of(panels):
            gram[pl.ds(pl.multiple_of(at + BLK * k, PIECE), size), BLK * c : BLK * (c + 1)] = piece[
                base : base + size, :]
            for part in range(0, size, PIECE):
                value = piece[base + part : base + part + PIECE, :].astype(jnp.float32)
                square = square + value * value * (1.0 if k == c else 2.0)
            base += size
    for k, c in blocks_of(panels):
        if k < c:
            gram[BLK * c : BLK * (c + 1), BLK * k : BLK * (k + 1)] = gram[
                BLK * k : BLK * (k + 1), BLK * c : BLK * (c + 1)].T
    return square


def unflatten(shape, refs):
    refs, out = list(refs), []
    for panels, size, pieces in shape:
        out.append((panels, size, refs[:pieces]))
        refs = refs[pieces:]
    return out


def early_kernel(shape, where, *refs):
    gram, square = refs[-2:]
    square[...] = sum(put_pieces(chunk, gram, where) for chunk in unflatten(shape, refs[:-2]))


def steps_kernel(shape, where, w_ref, mask_ref, old, square, *refs):
    pieces, (out, gram) = refs[:-2], refs[-2:]
    total = square[...] + sum(put_pieces(chunk, gram, where) for chunk in unflatten(shape, pieces))
    rate = step_scale / jnp.sqrt(jnp.sum(total) + 1e-06)
    dense = w_ref[...]
    keep = mask_ref[...].astype(jnp.float32)
    weights = keep * dense
    rows = dense.shape[0]
    for section in range(STEPS):
        change = weights - dense
        high = change.astype(jnp.bfloat16)
        low = (change - high.astype(jnp.float32)).astype(jnp.bfloat16)
        both = jnp.dot(jnp.concatenate([high, low], axis=0), gram[...], preferred_element_type=jnp.float32)
        weights = keep * (weights - rate * (both[0:rows] + both[rows:]))
    out[...] = weights


def call(kernel, outs, *args, scratch=(), smem=True, aliases={}):
    return pl.pallas_call(
        kernel, in_specs=[SMEM if smem and i == 0 else VMEM for i in range(len(args))],
        out_specs=[VMEM] * len(outs),
        out_shape=[jax.ShapeDtypeStruct(s, d) for s, d in outs],
        scratch_shapes=list(scratch), input_output_aliases=aliases,
        compiler_params=pltpu.CompilerParams(vmem_limit_bytes=16 << 20),
    )(*args)


def over(axis, bit):
    return lambda a: lax.ppermute(a, axis, [(i, i ^ bit) for i in range(4)])


def local_grams(plan, tokens, routes, w_orig, mask):
    toks, width = tokens.shape
    experts = lax.axis_size("expert")
    z, dp = lax.axis_index("expert"), lax.axis_index("dp")
    where = jnp.stack([z, dp // 2, dp % 2]).astype(jnp.int32)
    over_core, over_x = over("dp", 1), over("dp", 2)
    bf16, f32 = jnp.bfloat16, jnp.float32

    def lift(tok, routes_t):
        return call(functools.partial(lift_kernel, experts), [((2 * width, toks), bf16)],
                    where, tok, routes_t, scratch=[pltpu.VMEM((width, toks), bf16)])[0]

    other, other_routes = over_core(tokens), over_core(routes.T)
    lhs = lift(tokens, routes.T)
    other_lhs = lift(other, other_routes)
    def gram(panels, mode, at):
        blocks = count(panels)
        dims = (2, 2 * PIECE * blocks, BLK) if mode == "z" else (experts, PIECE * blocks, BLK)
        return call(functools.partial(gram_kernel, panels, mode, experts),
                    [(dims, f32), (dims, bf16)], at, lhs, tokens, other_lhs, other)

    def flat(panels, mode=""):
        return ((2 if mode == "z" else 1) * PIECE * count(panels), BLK)

    def summed(*parts):
        return call(sum_kernel, [(parts[0].shape, bf16)], *parts, smem=False)[0]

    over_z = [over("expert", bit) for bit in range(4)]
    chunk_a, chunk_z, chunk_b = plan
    keep_a, send_a = gram(chunk_a, "x", where)
    got_a = over_x(send_a)
    keep_z, send_z = gram(chunk_z, "z", after(where, send_a))
    near_z = over_z[1](send_z)
    keep_b, send_b = gram(chunk_b, "x", after(where, send_z))
    got_b = over_x(send_b)
    own_z, send_z = call(pair_kernel, [(flat(chunk_z, "z"), f32), (flat(chunk_z, "z"), bf16)],
                         keep_z, after(near_z, send_b), smem=False)
    far_z = over_z[2](send_z)

    def first_hop(panels, keep, got):
        keep, send = call(split_kernel, [((2,) + flat(panels), f32), ((2,) + flat(panels), bf16)],
                          keep, got, smem=False)
        return keep, over_z[1](send)

    def second_hop(panels, keep, near):
        own, send = call(pair_kernel, [(flat(panels), f32), (flat(panels), bf16)], keep, near, smem=False)
        return summed(own, over_z[2](send))

    own_a, near_a = first_hop(chunk_a, keep_a, after(got_a, send_b))
    own_b, near_b = first_hop(chunk_b, keep_b, got_b)
    part_z = summed(own_z, far_z)
    both_z = summed(part_z, over_x(part_z))
    final_a = second_hop(chunk_a, own_a, near_a)
    final_b = second_hop(chunk_b, own_b, near_b)
    x_a = over_x(final_a)
    x_b = over_x(final_b)
    shape = ((chunk_z, 2 * PIECE, 2), (chunk_a, PIECE, 4), (chunk_b, PIECE, 4))
    gram_early, square = call(functools.partial(early_kernel, shape[:2]),
                        [((width, width), bf16), ((PIECE, BLK), f32)],
                        where, both_z, over_core(both_z), final_a, over_core(final_a), x_a, over_core(x_a))
    last = [final_b, over_core(final_b), x_b, over_core(x_b)]
    out, _ = call(functools.partial(steps_kernel, shape[2:]),
                  [(w_orig.shape[1:], f32), ((width, width), bf16)],
                  where, w_orig[0], mask[0], gram_early, square, *last, aliases={3: 1})
    return out[None]


def after(value, earlier):
    return lax.optimization_barrier((value, earlier))[0]


PLAN = ((3,), (2,), (0, 1))


def solution(mesh):
    placed = (
        P(("groups", "expert", "dp"), None),
        P(("groups", "expert", "dp"), None),
        P("expert", "dp", None),
        P("expert", "dp", None),
    )
    few = mesh.shape["expert"] == 4 and mesh.shape["dp"] == 4
    local = functools.partial(local_grams, PLAN) if few else local_rows
    return jax.shard_map(
        local,
        mesh=mesh,
        in_specs=placed,
        out_specs=P(("groups", "expert"), "dp", None),
        check_vma=False,
    )
```

```python
import functools

import jax
import jax.numpy as jnp
from jax import lax
from jax.experimental import pallas as pl
from jax.experimental.pallas import tpu as pltpu
from jax.sharding import PartitionSpec as P

STEPS = 3


step_scale = 1.5

BLK = 128
PIECE = 32
VMEM = pl.BlockSpec(memory_space=pltpu.VMEM)
SMEM = pl.BlockSpec(memory_space=pltpu.SMEM)


def full_product(rows):
    return lax.dot_general(rows, rows, (((0,), (0,)), ((), ())), preferred_element_type=jnp.float32)


def local_rows(tokens, routes, w_orig, mask):
    experts_n = lax.axis_size("expert")
    tok_rows, topk_count = routes.shape
    width = tokens.shape[1]
    capacity = max(2, min(tok_rows, 5 * tok_rows * topk_count // (4 * experts_n)))
    flat_routes = routes.reshape(-1)
    onehot = (flat_routes[:, None] == jnp.arange(experts_n, dtype=jnp.int32)[None, :]).astype(
        jnp.int32
    )
    before = jnp.cumsum(onehot, axis=0) - onehot
    slot_index = jnp.sum(before * onehot, axis=1)
    target = flat_routes * capacity + slot_index
    source = jnp.arange(flat_routes.shape[0], dtype=jnp.int32) // topk_count
    buffer = jnp.zeros((experts_n * capacity, width), jnp.bfloat16).at[target].set(tokens[source])
    outgoing = buffer.reshape(experts_n, capacity, width)
    arrived = lax.all_to_all(outgoing, "expert", split_axis=0, concat_axis=0, tiled=True).reshape(
        experts_n * capacity, width
    )
    local_terms = full_product(arrived)
    gram_matrix = lax.psum(local_terms.astype(jnp.bfloat16), "dp").astype(jnp.float32)
    frobenius = jnp.sqrt(jnp.sum(gram_matrix * gram_matrix) + 1e-06)
    rate_value = step_scale / frobenius
    dense_copy = w_orig[0]
    keep_mask = mask[0].astype(jnp.float32)
    weights = keep_mask * dense_copy
    for section in range(STEPS):
        change = weights - dense_copy
        gradient = jnp.dot(
            change, gram_matrix, precision=lax.Precision.HIGHEST, preferred_element_type=jnp.float32
        )
        weights = keep_mask * (weights - rate_value * gradient)
    return weights[None]


def count(panels):
    return sum(4 * j + 3 for j in panels)


def blocks_of(panels):
    return [(k, c) for j in panels for c in (2 * j, 2 * j + 1) for k in range(c + 1)]


def flags_of(z, routes):
    numbers = jnp.arange(16, dtype=jnp.int32) ^ z
    return jnp.any(numbers[:, None, None] == routes.T[None], axis=1).astype(jnp.bfloat16)


def lift(where, experts, turned, flags, out, lanes):
    row = 64 * where[2]
    ats = (row + PIECE * where[1], row + PIECE * (1 - where[1]))
    first = 0
    for k in range(turned.shape[0] // BLK):
        for at in ats:
            rows = turned[pl.ds(pl.multiple_of(at + BLK * k, PIECE), PIECE), lanes]
            for e in range(experts):
                out[first : first + PIECE, lanes] = rows * flags[e : e + 1, lanes]
                first += PIECE


def own_kernel(panel, experts, where, tok, flags, lhs, part, turned):
    for i in range(tok.shape[0] // BLK):
        lanes = slice(BLK * i, BLK * (i + 1))
        turned[:, lanes] = tok[lanes, :].T
        lift(where, experts, turned, flags, lhs, lanes)
    part[...] = jnp.dot(lhs[0 : part.shape[0], :], tok[:, 256 * panel : 256 * panel + 256],
                        preferred_element_type=jnp.float32)


def pack(total, j, base, mode, experts, halves, keep, send):
    group = 2 * experts * PIECE
    for side in range(2):
        for k in range(2 * j + side + 1):
            for s in range(2):
                for e in range(experts):
                    first = group * k + experts * PIECE * s + PIECE * e
                    value = total[first : first + PIECE, BLK * side : BLK * (side + 1)]
                    if mode == "z":
                        out = keep if e % 2 == 0 else send
                        at = pl.multiple_of(halves[s] + base, PIECE)
                        out[e // 2, pl.ds(at, PIECE), :] = value.astype(out.dtype)
                    else:
                        out = (keep, send)[s]
                        out[e, base : base + PIECE, :] = value.astype(out.dtype)
            base += 2 * PIECE if mode == "z" else PIECE
    return base


def first_kernel(panel, experts, where, tok_b, flags, part, keep, send, lhs_b, turned):
    for i in range(tok_b.shape[0] // BLK):
        lanes = slice(BLK * i, BLK * (i + 1))
        turned[:, lanes] = tok_b[lanes, :].T
        lift(where, experts, turned, flags, lhs_b, lanes)
    total = part[...] + jnp.dot(lhs_b[0 : part.shape[0], :], tok_b[:, 256 * panel : 256 * panel + 256],
                                preferred_element_type=jnp.float32)
    pack(total, panel, 0, "x", experts, None, keep, send)


def gram_kernel(panels, mode, experts, where, lhs_a, tok_a, lhs_b, tok_b, keep, send):
    group = 2 * experts * PIECE
    halves = (PIECE * where[1], PIECE * (1 - where[1]))
    base = 0
    for j in panels:
        used, cols = slice(0, group * (2 * j + 2)), slice(256 * j, 256 * j + 256)
        total = jnp.dot(lhs_a[used, :], tok_a[:, cols], preferred_element_type=jnp.float32)
        total = total + jnp.dot(lhs_b[used, :], tok_b[:, cols], preferred_element_type=jnp.float32)
        base = pack(total, j, base, mode, experts, halves, keep, send)


def pair_kernel(keep, got, own, *outs):
    for e, out in enumerate((own,) + outs):
        out[...] = (keep[e] + got[e].astype(jnp.float32)).astype(out.dtype)


def split_kernel(keep, got, own, out):
    for e in range(4):
        to = (own, out)[e % 2]
        to[e // 2] = (keep[e] + got[e].astype(jnp.float32)).astype(to.dtype)


def sum_kernel(*refs):
    total = refs[0][...].astype(jnp.float32)
    for ref in refs[1:-1]:
        total = total + ref[...].astype(jnp.float32)
    refs[-1][...] = total.astype(refs[-1].dtype)


def put_pieces(chunk, gram, where):
    panels, size, pieces = chunk
    core, x = where[2], where[1]
    if size == PIECE:
        ats = [64 * a + PIECE * b for b in (x, 1 - x) for a in (core, 1 - core)]
    else:
        ats = [64 * a for a in (core, 1 - core)]
    square = jnp.zeros((PIECE, BLK), jnp.float32)
    for at, piece in zip(ats, pieces):
        base = 0
        for k, c in blocks_of(panels):
            gram[pl.ds(pl.multiple_of(at + BLK * k, PIECE), size), BLK * c : BLK * (c + 1)] = piece[
                base : base + size, :]
            for part in range(0, size, PIECE):
                value = piece[base + part : base + part + PIECE, :].astype(jnp.float32)
                square = square + value * value * (1.0 if k == c else 2.0)
            base += size
    for k, c in blocks_of(panels):
        if k < c:
            gram[BLK * c : BLK * (c + 1), BLK * k : BLK * (k + 1)] = gram[
                BLK * k : BLK * (k + 1), BLK * c : BLK * (c + 1)].T
    return square


def unflatten(shape, refs):
    refs, out = list(refs), []
    for panels, size, pieces in shape:
        out.append((panels, size, refs[:pieces]))
        refs = refs[pieces:]
    return out


def early_kernel(shape, where, *refs):
    gram, square = refs[-2:]
    square[...] = sum(put_pieces(chunk, gram, where) for chunk in unflatten(shape, refs[:-2]))


def steps_kernel(shape, where, w_ref, mask_ref, old, square, *refs):
    pieces, (out, gram) = refs[:-2], refs[-2:]
    total = square[...] + sum(put_pieces(chunk, gram, where) for chunk in unflatten(shape, pieces))
    rate = step_scale / jnp.sqrt(jnp.sum(total) + 1e-06)
    dense = w_ref[...]
    keep = mask_ref[...].astype(jnp.float32)
    weights = keep * dense
    rows = dense.shape[0]
    for section in range(STEPS):
        change = weights - dense
        high = change.astype(jnp.bfloat16)
        low = (change - high.astype(jnp.float32)).astype(jnp.bfloat16)
        both = jnp.dot(jnp.concatenate([high, low], axis=0), gram[...], preferred_element_type=jnp.float32)
        weights = keep * (weights - rate * (both[0:rows] + both[rows:]))
    out[...] = weights


def call(kernel, outs, *args, scratch=(), smem=True, aliases={}):
    return pl.pallas_call(
        kernel, in_specs=[SMEM if smem and i == 0 else VMEM for i in range(len(args))],
        out_specs=[VMEM] * len(outs),
        out_shape=[jax.ShapeDtypeStruct(s, d) for s, d in outs],
        scratch_shapes=list(scratch), input_output_aliases=aliases,
        compiler_params=pltpu.CompilerParams(vmem_limit_bytes=16 << 20),
    )(*args)


def over(axis, bit):
    return lambda a: lax.ppermute(a, axis, [(i, i ^ bit) for i in range(4)])


def local_grams(plan, tokens, routes, w_orig, mask):
    toks, width = tokens.shape
    experts = lax.axis_size("expert")
    z, dp = lax.axis_index("expert"), lax.axis_index("dp")
    where = jnp.stack([z, dp // 2, dp % 2]).astype(jnp.int32)
    over_core, over_x = over("dp", 1), over("dp", 2)
    bf16, f32 = jnp.bfloat16, jnp.float32

    over_z = [over("expert", bit) for bit in range(4)]
    chunk_a, chunk_z, chunk_b = plan
    panel, = chunk_a
    lifted, turned = ((2 * width, toks), bf16), pltpu.VMEM((width, toks), bf16)
    dims = (experts, PIECE * count(chunk_a), BLK)
    flags = flags_of(z, routes)
    other, other_flags = over_core(tokens), over_core(flags)
    lhs, part = call(
        functools.partial(own_kernel, panel, experts),
        [lifted, ((4 * experts * PIECE * (panel + 1), 256), f32)],
        where, tokens, flags, scratch=[turned])
    keep_a, send_a, other_lhs = call(
        functools.partial(first_kernel, panel, experts), [(dims, f32), (dims, bf16), lifted],
        where, other, other_flags, part, scratch=[turned])
    got_a = over_x(send_a)


    def gram(panels, mode, at):
        blocks = count(panels)
        dims = (2, 2 * PIECE * blocks, BLK) if mode == "z" else (experts, PIECE * blocks, BLK)
        return call(functools.partial(gram_kernel, panels, mode, experts),
                    [(dims, f32), (dims, bf16)], at, lhs, tokens, other_lhs, other)

    def flat(panels, mode=""):
        return ((2 if mode == "z" else 1) * PIECE * count(panels), BLK)

    def summed(*parts):
        return call(sum_kernel, [(parts[0].shape, bf16)], *parts, smem=False)[0]

    keep_z, send_z = gram(chunk_z, "z", after(where, send_a))
    near_z = over_z[1](send_z)
    keep_b, send_b = gram(chunk_b, "x", after(where, send_z))
    got_b = over_x(send_b)
    own_z, send_z = call(pair_kernel, [(flat(chunk_z, "z"), f32), (flat(chunk_z, "z"), bf16)],
                         keep_z, after(near_z, send_b), smem=False)
    far_z = over_z[2](send_z)

    def first_hop(panels, keep, got):
        keep, send = call(split_kernel, [((2,) + flat(panels), f32), ((2,) + flat(panels), bf16)],
                          keep, got, smem=False)
        return keep, over_z[1](send)

    def second_hop(panels, keep, near):
        own, send = call(pair_kernel, [(flat(panels), f32), (flat(panels), bf16)], keep, near, smem=False)
        return summed(own, over_z[2](send))

    own_a, near_a = first_hop(chunk_a, keep_a, after(got_a, send_b))
    own_b, near_b = first_hop(chunk_b, keep_b, got_b)
    part_z = summed(own_z, far_z)
    both_z = summed(part_z, over_x(part_z))
    final_a = second_hop(chunk_a, own_a, near_a)
    final_b = second_hop(chunk_b, own_b, near_b)
    x_a = over_x(final_a)
    x_b = over_x(final_b)
    shape = ((chunk_z, 2 * PIECE, 2), (chunk_a, PIECE, 4), (chunk_b, PIECE, 4))
    outs = [((width, width), bf16), ((PIECE, BLK), f32)]
    of_z = [both_z, over_core(both_z)]
    of_a = [final_a, over_core(final_a), x_a, over_core(x_a)]
    gram_early, square = call(functools.partial(early_kernel, shape[:2]), outs, where, *of_z, *of_a)
    last = [final_b, over_core(final_b), x_b, over_core(x_b)]
    out, _ = call(functools.partial(steps_kernel, shape[2:]),
                  [(w_orig.shape[1:], f32), ((width, width), bf16)],
                  where, w_orig[0], mask[0], gram_early, square, *last, aliases={3: 1})
    return out[None]


def after(value, earlier):
    return lax.optimization_barrier((value, earlier))[0]


PLAN = ((3,), (2,), (0, 1))


def solution(mesh):
    placed = (
        P(("groups", "expert", "dp"), None),
        P(("groups", "expert", "dp"), None),
        P("expert", "dp", None),
        P("expert", "dp", None),
    )
    few = mesh.shape["expert"] == 4 and mesh.shape["dp"] == 4
    local = functools.partial(local_grams, PLAN) if few else local_rows
    return jax.shard_map(
        local,
        mesh=mesh,
        in_specs=placed,
        out_specs=P(("groups", "expert"), "dp", None),
        check_vma=False,
    )
```

```python
import functools

import jax
import jax.numpy as jnp
from jax import lax
from jax.experimental import pallas as pl
from jax.experimental.pallas import tpu as pltpu
from jax.sharding import PartitionSpec as P

STEPS = 3


step_scale = 1.5

BLK = 128
PIECE = 32
VMEM = pl.BlockSpec(memory_space=pltpu.VMEM)
SMEM = pl.BlockSpec(memory_space=pltpu.SMEM)


def full_product(rows):
    return lax.dot_general(rows, rows, (((0,), (0,)), ((), ())), preferred_element_type=jnp.float32)


def local_rows(tokens, routes, w_orig, mask):
    experts_n = lax.axis_size("expert")
    tok_rows, topk_count = routes.shape
    width = tokens.shape[1]
    capacity = max(2, min(tok_rows, 5 * tok_rows * topk_count // (4 * experts_n)))
    flat_routes = routes.reshape(-1)
    onehot = (flat_routes[:, None] == jnp.arange(experts_n, dtype=jnp.int32)[None, :]).astype(
        jnp.int32
    )
    before = jnp.cumsum(onehot, axis=0) - onehot
    slot_index = jnp.sum(before * onehot, axis=1)
    target = flat_routes * capacity + slot_index
    source = jnp.arange(flat_routes.shape[0], dtype=jnp.int32) // topk_count
    buffer = jnp.zeros((experts_n * capacity, width), jnp.bfloat16).at[target].set(tokens[source])
    outgoing = buffer.reshape(experts_n, capacity, width)
    arrived = lax.all_to_all(outgoing, "expert", split_axis=0, concat_axis=0, tiled=True).reshape(
        experts_n * capacity, width
    )
    local_terms = full_product(arrived)
    gram_matrix = lax.psum(local_terms.astype(jnp.bfloat16), "dp").astype(jnp.float32)
    frobenius = jnp.sqrt(jnp.sum(gram_matrix * gram_matrix) + 1e-06)
    rate_value = step_scale / frobenius
    dense_copy = w_orig[0]
    keep_mask = mask[0].astype(jnp.float32)
    weights = keep_mask * dense_copy
    for section in range(STEPS):
        change = weights - dense_copy
        gradient = jnp.dot(
            change, gram_matrix, precision=lax.Precision.HIGHEST, preferred_element_type=jnp.float32
        )
        weights = keep_mask * (weights - rate_value * gradient)
    return weights[None]


EXTRA = 16


def blocks_of(panels):
    return [(k, c) for j in panels for c in (2 * j, 2 * j + 1) for k in range(2 * j + 1)]


def rows_of(panels, size):
    return size * len(blocks_of(panels)) + EXTRA + MORE.get((panels, size), 0)


def flags_of(z, routes):
    numbers = jnp.arange(16, dtype=jnp.int32) ^ z
    return jnp.any(numbers[:, None, None] == routes.T[None], axis=1).astype(jnp.bfloat16)


def lift(where, experts, turned, flags, out, lanes):
    row = 64 * where[2]
    ats = (row + PIECE * where[1], row + PIECE * (1 - where[1]))
    first = 0
    for k in range(turned.shape[0] // BLK):
        for at in ats:
            rows = turned[pl.ds(pl.multiple_of(at + BLK * k, PIECE), PIECE), lanes]
            for e in range(experts):
                out[first : first + PIECE, lanes] = rows * flags[e : e + 1, lanes]
                first += PIECE


def own_kernel(panel, experts, where, tok, flags, lhs, part, turned):
    for i in range(tok.shape[0] // BLK):
        lanes = slice(BLK * i, BLK * (i + 1))
        turned[:, lanes] = tok[lanes, :].T
        lift(where, experts, turned, flags, lhs, lanes)
    part[...] = jnp.dot(lhs[0 : part.shape[0], :], tok[:, 256 * panel : 256 * panel + 256],
                        preferred_element_type=jnp.float32)


def pack(totals, panels, mode, experts, where, keep, send):
    group = 2 * experts * PIECE
    size = 2 * PIECE if mode == "z" else PIECE
    halves = (PIECE * where[1], PIECE * (1 - where[1]))
    col = lax.broadcasted_iota(jnp.int32, (PIECE, BLK), 1)
    row = lax.broadcasted_iota(jnp.int32, (PIECE, BLK), 0) + 64 * where[2]
    end = size * len(blocks_of(panels))
    for e in range(experts):
        lines = []
        for s in range(2):
            if mode == "z":
                out, lead, shift = (keep, send)[e % 2], e // 2, halves[s]
            else:
                out, lead, shift = (keep, send)[s], e, 0
            base, lines_s = 0, []
            for total, j in zip(totals, panels):
                for side in range(2):
                    for k in range(2 * j + 1):
                        first = group * k + experts * PIECE * s + PIECE * e
                        value = total[first : first + PIECE, BLK * side : BLK * (side + 1)]
                        if side == 0 and k == 2 * j:
                            below = total[first + group : first + group + PIECE, BLK : 2 * BLK]
                            at = row + halves[s]
                            value = jnp.where(col >= at, value, below)
                            lines_s.append(jnp.sum(jnp.where(col == at, below, 0.0), axis=0, keepdims=True))
                        spot = pl.multiple_of(shift + base, PIECE) if mode == "z" else base
                        out[lead, pl.ds(spot, PIECE), :] = value.astype(out.dtype)
                        base += size
            lines.append(lines_s)
        if mode == "z":
            slabs = [((keep, send)[e % 2], e // 2, [a + b for a, b in zip(*lines)])]
        else:
            slabs = [(keep, e, lines[0]), (send, e, lines[1])]
        for out, lead, slab in slabs:
            slab = slab + [jnp.zeros((out.shape[1] - end - len(slab), BLK), jnp.float32)]
            out[lead, end:, :] = jnp.concatenate(slab, axis=0).astype(out.dtype)


def first_kernel(panel, experts, where, tok_b, flags, part, keep, send, lhs_b, turned):
    for i in range(tok_b.shape[0] // BLK):
        lanes = slice(BLK * i, BLK * (i + 1))
        turned[:, lanes] = tok_b[lanes, :].T
        lift(where, experts, turned, flags, lhs_b, lanes)
    total = part[...] + jnp.dot(lhs_b[0 : part.shape[0], :], tok_b[:, 256 * panel : 256 * panel + 256],
                                preferred_element_type=jnp.float32)
    pack([total], (panel,), "x", experts, where, keep, send)


def gram_kernel(panels, mode, experts, where, lhs_a, tok_a, lhs_b, tok_b, keep, send):
    group = 2 * experts * PIECE
    totals = []
    for j in panels:
        used, cols = slice(0, group * (2 * j + 2)), slice(256 * j, 256 * j + 256)
        total = jnp.dot(lhs_a[used, :], tok_a[:, cols], preferred_element_type=jnp.float32)
        totals.append(total + jnp.dot(lhs_b[used, :], tok_b[:, cols], preferred_element_type=jnp.float32))
    pack(totals, panels, mode, experts, where, keep, send)


def pair_kernel(keep, got, own, *outs):
    for e, out in enumerate((own,) + outs):
        out[...] = (keep[e] + got[e].astype(jnp.float32)).astype(out.dtype)


def split_kernel(keep, got, own, out):
    for e in range(4):
        to = (own, out)[e % 2]
        to[e // 2] = (keep[e] + got[e].astype(jnp.float32)).astype(to.dtype)


def sum_kernel(*refs):
    total = refs[0][...].astype(jnp.float32)
    for ref in refs[1:-1]:
        total = total + ref[...].astype(jnp.float32)
    refs[-1][...] = total.astype(refs[-1].dtype)


def put_pieces(chunk, gram, where):
    panels, size, pieces = chunk
    core, x = where[2], where[1]
    if size == PIECE:
        ats = [64 * a + PIECE * b for b in (x, 1 - x) for a in (core, 1 - core)]
    else:
        ats = [64 * a for a in (core, 1 - core)]
    square = jnp.zeros((PIECE, BLK), jnp.float32)
    end = size * len(blocks_of(panels))
    for at, piece in zip(ats, pieces):
        base = 0
        for k, c in blocks_of(panels):
            gram[pl.ds(pl.multiple_of(at + BLK * k, PIECE), size), BLK * c : BLK * (c + 1)] = piece[
                base : base + size, :]
            for part in range(0, size, PIECE):
                if k < c:
                    value = piece[base + part : base + part + PIECE, :].astype(jnp.float32)
                    square = square + 2.0 * value * value
            base += size
    for k, c in blocks_of(panels):
        if k < c:
            gram[BLK * c : BLK * (c + 1), BLK * k : BLK * (k + 1)] = gram[
                BLK * k : BLK * (k + 1), BLK * c : BLK * (c + 1)].T
    lines = sum(piece[end : end + EXTRA, :].astype(jnp.float32) for piece in pieces)
    col = lax.broadcasted_iota(jnp.int32, (BLK, BLK), 1)
    row = lax.broadcasted_iota(jnp.int32, (BLK, BLK), 0)
    for i, j in enumerate(panels):
        first, second = slice(256 * j, 256 * j + BLK), slice(256 * j + BLK, 256 * j + 256)
        mixed = gram[first, first].astype(jnp.float32)
        turned = mixed.T
        upper = jnp.where(col >= row, mixed, turned)
        lower = jnp.where(col < row, mixed, jnp.where(col > row, turned, lines[i : i + 1, :]))
        gram[first, first] = upper.astype(gram.dtype)
        gram[second, second] = lower.astype(gram.dtype)
        both = upper * upper + lower * lower
        for part in range(0, BLK, PIECE):
            square = square + both[part : part + PIECE, :]
    return square


def unflatten(shape, refs):
    refs, out = list(refs), []
    for panels, size, pieces in shape:
        out.append((panels, size, refs[:pieces]))
        refs = refs[pieces:]
    return out


def early_kernel(shape, where, *refs):
    gram, square = refs[-2:]
    square[...] = sum(put_pieces(chunk, gram, where) for chunk in unflatten(shape, refs[:-2]))


def steps_kernel(shape, where, w_ref, mask_ref, old, square, *refs):
    pieces, (out, gram) = refs[:-2], refs[-2:]
    total = square[...] + sum(put_pieces(chunk, gram, where) for chunk in unflatten(shape, pieces))
    rate = step_scale / jnp.sqrt(jnp.sum(total) + 1e-06)
    dense = w_ref[...]
    keep = mask_ref[...].astype(jnp.float32)
    weights = keep * dense
    rows = dense.shape[0]
    for section in range(STEPS):
        change = weights - dense
        high = change.astype(jnp.bfloat16)
        low = (change - high.astype(jnp.float32)).astype(jnp.bfloat16)
        both = jnp.dot(jnp.concatenate([high, low], axis=0), gram[...], preferred_element_type=jnp.float32)
        weights = keep * (weights - rate * (both[0:rows] + both[rows:]))
    out[...] = weights


def call(kernel, outs, *args, scratch=(), smem=True, aliases={}):
    return pl.pallas_call(
        kernel, in_specs=[SMEM if smem and i == 0 else VMEM for i in range(len(args))],
        out_specs=[VMEM] * len(outs),
        out_shape=[jax.ShapeDtypeStruct(s, d) for s, d in outs],
        scratch_shapes=list(scratch), input_output_aliases=aliases,
        compiler_params=pltpu.CompilerParams(vmem_limit_bytes=16 << 20),
    )(*args)


def over(axis, bit):
    return lambda a: lax.ppermute(a, axis, [(i, i ^ bit) for i in range(4)])


def local_grams(plan, tokens, routes, w_orig, mask):
    toks, width = tokens.shape
    experts = lax.axis_size("expert")
    z, dp = lax.axis_index("expert"), lax.axis_index("dp")
    where = jnp.stack([z, dp // 2, dp % 2]).astype(jnp.int32)
    over_core, over_x = over("dp", 1), over("dp", 2)
    bf16, f32 = jnp.bfloat16, jnp.float32

    over_z = [over("expert", bit) for bit in range(4)]
    chunk_a, chunk_z, chunk_b = plan
    panel, = chunk_a
    lifted, turned = ((2 * width, toks), bf16), pltpu.VMEM((width, toks), bf16)
    dims = (experts, rows_of(chunk_a, PIECE), BLK)
    flags = flags_of(z, routes)
    other, other_flags = over_core(tokens), over_core(flags)
    lhs, part = call(
        functools.partial(own_kernel, panel, experts),
        [lifted, ((4 * experts * PIECE * (panel + 1), 256), f32)],
        where, tokens, flags, scratch=[turned])
    keep_a, send_a, other_lhs = call(
        functools.partial(first_kernel, panel, experts), [(dims, f32), (dims, bf16), lifted],
        where, other, other_flags, part, scratch=[turned])
    got_a = over_x(send_a)


    def gram(panels, mode, at):
        dims = (2 if mode == "z" else experts,) + flat(panels, mode)
        return call(functools.partial(gram_kernel, panels, mode, experts),
                    [(dims, f32), (dims, bf16)], at, lhs, tokens, other_lhs, other)

    def flat(panels, mode=""):
        return (rows_of(panels, 2 * PIECE if mode == "z" else PIECE), BLK)

    def summed(*parts):
        return call(sum_kernel, [(parts[0].shape, bf16)], *parts, smem=False)[0]

    keep_z, send_z = gram(chunk_z, "z", after(where, send_a))
    near_z = over_z[1](send_z)
    keep_b, send_b = gram(chunk_b, "x", after(where, send_z))
    got_b = over_x(send_b)
    own_z, send_z = call(pair_kernel, [(flat(chunk_z, "z"), f32), (flat(chunk_z, "z"), bf16)],
                         keep_z, after(near_z, send_b), smem=False)
    far_z = over_z[2](send_z)

    def first_hop(panels, keep, got):
        keep, send = call(split_kernel, [((2,) + flat(panels), f32), ((2,) + flat(panels), bf16)],
                          keep, got, smem=False)
        return keep, over_z[1](send)

    def second_hop(panels, keep, near):
        own, send = call(pair_kernel, [(flat(panels), f32), (flat(panels), bf16)], keep, near, smem=False)
        return summed(own, over_z[2](send))

    own_a, near_a = first_hop(chunk_a, keep_a, after(got_a, send_b))
    own_b, near_b = first_hop(chunk_b, keep_b, got_b)
    part_z = summed(own_z, far_z)
    both_z = summed(part_z, over_x(part_z))
    final_a = second_hop(chunk_a, own_a, near_a)
    final_b = second_hop(chunk_b, own_b, near_b)
    x_a = over_x(final_a)
    x_b = over_x(final_b)
    shape = ((chunk_z, 2 * PIECE, 2), (chunk_a, PIECE, 4), (chunk_b, PIECE, 4))
    outs = [((width, width), bf16), ((PIECE, BLK), f32)]
    of_z = [both_z, over_core(both_z)]
    of_a = [final_a, over_core(final_a), x_a, over_core(x_a)]
    gram_early, square = call(functools.partial(early_kernel, shape[:2]), outs, where, *of_z, *of_a)
    last = [final_b, over_core(final_b), x_b, over_core(x_b)]
    out, _ = call(functools.partial(steps_kernel, shape[2:]),
                  [(w_orig.shape[1:], f32), ((width, width), bf16)],
                  where, w_orig[0], mask[0], gram_early, square, *last, aliases={3: 1})
    return out[None]


def after(value, earlier):
    return lax.optimization_barrier((value, earlier))[0]


MORE = {((0, 1), PIECE): 48}
PLAN = ((3,), (2,), (0, 1))


def solution(mesh):
    placed = (
        P(("groups", "expert", "dp"), None),
        P(("groups", "expert", "dp"), None),
        P("expert", "dp", None),
        P("expert", "dp", None),
    )
    few = mesh.shape["expert"] == 4 and mesh.shape["dp"] == 4
    local = functools.partial(local_grams, PLAN) if few else local_rows
    return jax.shard_map(
        local,
        mesh=mesh,
        in_specs=placed,
        out_specs=P(("groups", "expert"), "dp", None),
        check_vma=False,
    )
```
